32 devices in a mesh: layer: 8 (over z, y), plane: 4 (over x, core).
Axes of the slice: x: 2, y: 2, z: 4, core: 2. Of those that a mesh axis runs over, the one named last changes fastest.
Arguments:
- rhs_field: float32 [8, 2, 4, 32, 1024], P('layer', None, None, None, 'plane'), may hold values from -6 to 6
- panel_inverse: bfloat16 [8, 1024, 2048], P('layer'), may hold values from -1 to 1
- coupling: float32 [8, 2, 4, 32], P('layer', None, None, 'plane'), may hold values from -0.98 to 0.98, as said below
Outputs:
- sweep_field: float32 [8, 2, 4, 32, 1024], P('layer', None, None, None, 'plane')
The draws below stay inside these ranges and needn't reach their ends.
Inputs may be any that keep to these rules, and one draw needn't show every extreme that they name: Every complex coupling has modulus at most 0.98.
All inputs are finite; a program needn't handle non-finite values.
Results may differ from the reference program's by a relative error of at most 0.025.
Values may be sent and summed in bfloat16 or wider, within the bound.
A program may use at most 64 MiB of HBM per device.

```python
import math
import jax
import jax.numpy as jnp
from jax import lax

NX = 1024
LOAD_VECTORS = 4
LATERAL_POINTS = 32
DEPTH_SLABS = 8


def draw_panel_inverse(key, part):
    first = jax.random.fold_in(key, 0)
    spread = 0.5 / math.sqrt(2.0 * NX)
    noise = jax.random.truncated_normal(first, -4.0, 4.0, (DEPTH_SLABS, 2, NX, NX), jnp.float32)
    scale = 1.0 / math.sqrt(1.25)
    eye = jnp.eye(NX, dtype=jnp.float32)
    real = jnp.clip(scale * (eye + spread * noise[:, 0]), -1.0, 1.0)
    imag = scale * spread * noise[:, 1]
    return jnp.concatenate([real, imag], axis=2).astype(jnp.bfloat16)


def draw_coupling(key, part):
    first, second, final_portion, fourth = jax.random.split(key, 4)
    starting_position = jnp.exp(jax.random.uniform(first, (1, 1, LOAD_VECTORS, LATERAL_POINTS), jnp.float32, math.log(0.25), math.log(0.98)))
    match_tally = jax.random.randint(second, (DEPTH_SLABS, 1, LOAD_VECTORS, LATERAL_POINTS), 0, DEPTH_SLABS) < 2
    contiguous_span = jnp.where(match_tally, jax.random.uniform(final_portion, (DEPTH_SLABS, 1, LOAD_VECTORS, LATERAL_POINTS), jnp.float32, 0.5, 0.8), 1.0)
    phase = jax.random.uniform(fourth, (DEPTH_SLABS, 1, LOAD_VECTORS, LATERAL_POINTS), jnp.float32, -math.pi, math.pi)
    cyclic_period = starting_position * contiguous_span
    return jnp.concatenate([cyclic_period * jnp.cos(phase), cyclic_period * jnp.sin(phase)], axis=1)


def level_of(rng, dims, pieces, least, high):
    loudness = 1.0
    for axis_at, parts in pieces:
        steps = jax.random.uniform(jax.random.fold_in(jax.random.fold_in(rng, 6), axis_at), (parts,), jnp.float32, least / len(pieces), high / len(pieces))
        loudness = loudness * jnp.repeat(jnp.exp(steps), dims[axis_at] // parts).reshape((-1,) + (1,) * (len(dims) - 1 - axis_at))
    return loudness


def scatter_about(own_key, extent, deviation, limit, shards=(), kind=jnp.bfloat16):
    loudness = level_of(own_key, extent, shards, -0.22, 0.18) if shards else 1.0
    values = jax.random.normal(own_key, extent, jnp.float32) * deviation * loudness
    return jnp.minimum(jnp.maximum(values, -limit), limit).astype(kind)


def setup_inputs(seed: int = 0) -> dict:
    seeds = jax.random.split(jax.random.key(seed), 4)
    rhs_field = scatter_about(seeds[0], (DEPTH_SLABS, 2, LOAD_VECTORS, LATERAL_POINTS, NX), 1.0, 6.0, ((0, 8), (4, 4)), jnp.float32)
    panel_inverse = draw_panel_inverse(jax.random.fold_in(seeds[3], 71), 0)
    coupling = draw_coupling(jax.random.fold_in(seeds[3], 71), 0)
    return dict(rhs_field=rhs_field, panel_inverse=panel_inverse, coupling=coupling)


def complex_product(rows, inverse, width):
    flat = rows.reshape(-1, width)
    product = jnp.dot(flat, inverse, preferred_element_type=jnp.float32)
    product = product.reshape(rows.shape[:-1] + (2 * width,))
    real = product[0, ..., :width] - product[1, ..., width:]
    imag = product[0, ..., width:] + product[1, ..., :width]
    return jnp.stack([real, imag])


def twist(factor, field):
    real = factor[0] * field[0] - factor[1] * field[1]
    imag = factor[0] * field[1] + factor[1] * field[0]
    return jnp.stack([real, imag])


def reference(rhs_field, panel_inverse, coupling):
    factors = coupling[..., None]
    start = jnp.zeros(rhs_field.shape[1:], jnp.bfloat16)

    def forward(carried, inputs):
        source, inverse, factor = inputs
        mixed = (source + twist(factor, carried.astype(jnp.float32))).astype(jnp.bfloat16)
        result = complex_product(mixed, inverse, NX)
        return result.astype(jnp.bfloat16), result

    _, forward_all = lax.scan(forward, start, (rhs_field, panel_inverse, factors))

    def backward(carried, inputs):
        starting_position, inverse, factor = inputs
        result = starting_position + complex_product(carried, inverse, NX)
        return twist(factor, result).astype(jnp.bfloat16), result

    _, sweep_field = lax.scan(backward, start, (forward_all, panel_inverse, factors), reverse=True)
    return sweep_field
```

```python
import functools

import jax
import jax.numpy as jnp
from jax import lax
from jax.experimental import pallas as pl
from jax.experimental.pallas import tpu as pltpu
from jax.sharding import PartitionSpec as P

MESH = pl.DeviceIdType.MESH
GROUP = 1


def kernel(layers, planes, rhs, inverse_hbm, coupling, out, inverse, stage, lines, factors, ahead, ahead_out,
           behind, behind_out, forward, out_stage, out_in, inverse_sem, in_send, in_recv, ahead_send, ahead_recv,
           behind_send, behind_recv, out_send, out_recv):
    place = lax.axis_index("layer")
    mine = lax.axis_index("plane")
    last = layers - 1
    loads = rhs.shape[2]
    cells = coupling.shape[3]
    width = inverse.shape[0]
    part = rhs.shape[4]
    rows = 2 * cells
    blocks = loads // GROUP

    load_inverse = pltpu.make_async_copy(inverse_hbm.at[0], inverse, inverse_sem)
    load_inverse.start()

    barrier = pltpu.get_barrier_semaphore()
    peers = [lax.rem(mine + s, planes) for s in range(1, planes)]
    for peer in peers:
        pl.semaphore_signal(barrier, inc=1, device_id=(place, peer), device_id_type=MESH)

    @pl.when(place > 0)
    def _():
        pl.semaphore_signal(barrier, inc=1, device_id=(place - 1, mine), device_id_type=MESH)

    @pl.when(place < last)
    def _():
        pl.semaphore_signal(barrier, inc=1, device_id=(place + 1, mine), device_id_type=MESH)

    for p in range(planes):
        for r in range(loads):
            piece = rhs[0, :, r, p * cells:(p + 1) * cells, :].reshape(rows, part)
            stage[p, r] = piece.astype(jnp.bfloat16)

    @pl.when(place == 0)
    def _():
        ahead[...] = jnp.zeros_like(ahead)

    eye = lax.broadcasted_iota(jnp.int32, (cells, cells), 0) == lax.broadcasted_iota(jnp.int32, (cells, cells), 1)
    for c in range(2):
        for r in range(loads):
            row = jnp.broadcast_to(coupling[0, c, r:r + 1, :], (cells, cells))
            column = jnp.sum(jnp.where(eye, row, 0.0), axis=1, keepdims=True)
            factors[c, r] = jnp.broadcast_to(column, (cells, 128))

    pl.semaphore_wait(barrier, planes - 1 + jnp.where(place > 0, 1, 0) + jnp.where(place < last, 1, 0))

    def spread(r, s, source, target, send, recv):
        return pltpu.make_async_remote_copy(
            src_ref=source.at[peers[s], r], dst_ref=target.at[mine, r],
            send_sem=send.at[r, s], recv_sem=recv.at[r, s],
            device_id=(place, peers[s]), device_id_type=MESH)

    def sweep(b, source, target, send, recv, step):
        return pltpu.make_async_remote_copy(
            src_ref=source.at[b], dst_ref=target.at[b],
            send_sem=send.at[b], recv_sem=recv.at[b],
            device_id=(place + step, mine), device_id_type=MESH)

    for r in range(loads):
        for s in range(planes - 1):
            spread(r, s, stage, lines, in_send, in_recv).start()
        lines[mine, r] = stage[mine, r]

    def product(operand):
        flat = jnp.dot(operand, inverse[...], preferred_element_type=jnp.float32)
        flat = flat.reshape(GROUP, 2, cells, 2 * width)
        real = flat[:, 0, :, :width] - flat[:, 1, :, width:]
        imag = flat[:, 0, :, width:] + flat[:, 1, :, :width]
        return real, imag

    def pack(real, imag):
        return jnp.stack([real, imag], axis=1).reshape(GROUP * rows, width)

    def twist(b, real, imag):
        group = pl.ds(b * GROUP, GROUP)
        a = jnp.tile(factors[0, group], (1, 1, width // 128))
        c = jnp.tile(factors[1, group], (1, 1, width // 128))
        return a * real - c * imag, a * imag + c * real

    def split(flat):
        parts = flat.astype(jnp.float32).reshape(GROUP, 2, cells, width)
        return parts[:, 0], parts[:, 1]

    def finish(b, field):
        for r in range(b * GROUP, (b + 1) * GROUP):
            at = (r - b * GROUP) * rows
            for p in range(planes):
                out_stage[p, r] = field[at:at + rows, p * part:(p + 1) * part].astype(jnp.bfloat16)
            for s in range(planes - 1):
                spread(r, s, out_stage, out_in, out_send, out_recv).start()

    for b in range(blocks):
        for r in range(b * GROUP, (b + 1) * GROUP):
            for s in range(planes - 1):
                spread(r, s, stage, lines, in_send, in_recv).wait_recv()
        source = jnp.concatenate(
            [lines[p, b * GROUP:(b + 1) * GROUP].reshape(GROUP * rows, part) for p in range(planes)], axis=1)
        source_real, source_imag = split(source)

        @pl.when(place > 0)
        def _():
            sweep(b, ahead_out, ahead, ahead_send, ahead_recv, 1).wait_recv()

        real, imag = twist(b, *split(ahead[b]))
        mixed = pack(source_real + real, source_imag + imag).astype(jnp.bfloat16)
        if b == 0:
            load_inverse.wait()
        real, imag = product(mixed)
        result = pack(real, imag)
        forward[b] = result

        @pl.when(place < last)
        def _():
            ahead_out[b] = result.astype(jnp.bfloat16)
            sweep(b, ahead_out, ahead, ahead_send, ahead_recv, 1).start()

        @pl.when(place == last)
        def _():
            behind_out[b] = pack(*twist(b, real, imag)).astype(jnp.bfloat16)
            sweep(b, behind_out, behind, behind_send, behind_recv, -1).start()
            finish(b, result)

    @pl.when(place < last)
    def _():
        for b in range(blocks):
            first_real, first_imag = split(forward[b])
            sweep(b, behind_out, behind, behind_send, behind_recv, -1).wait_recv()
            real, imag = product(behind[b])
            real, imag = first_real + real, first_imag + imag

            @pl.when(place > 0)
            def _():
                behind_out[b] = pack(*twist(b, real, imag)).astype(jnp.bfloat16)
                sweep(b, behind_out, behind, behind_send, behind_recv, -1).start()

            finish(b, pack(real, imag))

    out_in[mine] = out_stage[mine]
    for r in range(loads):
        for s in range(planes - 1):
            spread(r, s, out_stage, out_in, out_send, out_recv).wait_recv()
        for p in range(planes):
            out[0, :, r, p * cells:(p + 1) * cells, :] = out_in[p, r].astype(jnp.float32).reshape(2, cells, part)

    for r in range(loads):
        for s in range(planes - 1):
            spread(r, s, stage, lines, in_send, in_recv).wait_send()
            spread(r, s, out_stage, out_in, out_send, out_recv).wait_send()

    @pl.when(place < last)
    def _():
        for b in range(blocks):
            sweep(b, ahead_out, ahead, ahead_send, ahead_recv, 1).wait_send()

    @pl.when(place > 0)
    def _():
        for b in range(blocks):
            sweep(b, behind_out, behind, behind_send, behind_recv, -1).wait_send()


def body(rhs_field, panel_inverse, coupling):
    layers, planes = lax.axis_size("layer"), lax.axis_size("plane")
    loads, part = rhs_field.shape[2], rhs_field.shape[4]
    width = panel_inverse.shape[1]
    cells = coupling.shape[3]
    rows = 2 * cells
    blocks = loads // GROUP
    exchange = pltpu.VMEM((planes, loads, rows, part), jnp.bfloat16)
    hop = pltpu.VMEM((blocks, GROUP * rows, width), jnp.bfloat16)
    per_peer = pltpu.SemaphoreType.DMA((loads, planes - 1))
    per_block = pltpu.SemaphoreType.DMA((blocks,))
    vmem = pl.BlockSpec(memory_space=pltpu.VMEM)
    return pl.pallas_call(
        functools.partial(kernel, layers, planes),
        out_shape=jax.ShapeDtypeStruct(rhs_field.shape, jnp.float32),
        in_specs=[vmem, pl.BlockSpec(memory_space=pl.ANY), vmem],
        out_specs=vmem,
        scratch_shapes=[
            pltpu.VMEM(panel_inverse.shape[1:], jnp.bfloat16),
            exchange,
            exchange,
            pltpu.VMEM((2, loads, cells, 128), jnp.float32),
            hop,
            hop,
            hop,
            hop,
            pltpu.VMEM((blocks, GROUP * rows, width), jnp.float32),
            exchange,
            exchange,
            pltpu.SemaphoreType.DMA,
            per_peer,
            per_peer,
            per_block,
            per_block,
            per_block,
            per_block,
            per_peer,
            per_peer,
        ],
        compiler_params=pltpu.CompilerParams(
            collective_id=0, has_side_effects=True, vmem_limit_bytes=60 * 1024 * 1024),
    )(rhs_field, panel_inverse, coupling)


def solution(mesh):
    in_specs = (
        P("layer", None, None, None, "plane"),
        P("layer", None, None),
        P("layer", None, None, "plane"),
    )
    out_specs = P("layer", None, None, None, "plane")
    return jax.shard_map(body, mesh=mesh, in_specs=in_specs, out_specs=out_specs, check_vma=False)
```

```python
import functools

import jax
import jax.numpy as jnp
from jax import lax
from jax.experimental import pallas as pl
from jax.experimental.pallas import tpu as pltpu
from jax.sharding import PartitionSpec as P

MESH = pl.DeviceIdType.MESH
CHUNKS = 2


def kernel(layers, planes, rhs, inverse_hbm, coupling, out, inverse, stage, lines, factors, ahead, ahead_out,
           behind, behind_out, forward, out_stage, out_in, inverse_sem, in_send, in_recv, ahead_send, ahead_recv,
           behind_send, behind_recv, out_send, out_recv):
    place = lax.axis_index("layer")
    mine = lax.axis_index("plane")
    last = layers - 1
    loads = rhs.shape[2]
    cells = coupling.shape[3]
    width = inverse.shape[0]
    part = rhs.shape[4]
    rows = 2 * cells

    load_inverse = pltpu.make_async_copy(inverse_hbm.at[0], inverse, inverse_sem)
    load_inverse.start()

    barrier = pltpu.get_barrier_semaphore()
    peers = [lax.rem(mine + s, planes) for s in range(1, planes)]
    for peer in peers:
        pl.semaphore_signal(barrier, inc=1, device_id=(place, peer), device_id_type=MESH)

    @pl.when(place > 0)
    def _():
        pl.semaphore_signal(barrier, inc=1, device_id=(place - 1, mine), device_id_type=MESH)

    @pl.when(place < last)
    def _():
        pl.semaphore_signal(barrier, inc=1, device_id=(place + 1, mine), device_id_type=MESH)

    for p in range(planes):
        for r in range(loads):
            piece = rhs[0, :, r, p * cells:(p + 1) * cells, :].reshape(rows, part)
            stage[p, r] = piece.astype(jnp.bfloat16)

    eye = lax.broadcasted_iota(jnp.int32, (cells, cells), 0) == lax.broadcasted_iota(jnp.int32, (cells, cells), 1)
    for c in range(2):
        for r in range(loads):
            row = jnp.broadcast_to(coupling[0, c, r:r + 1, :], (cells, cells))
            column = jnp.sum(jnp.where(eye, row, 0.0), axis=1, keepdims=True)
            factors[c, r] = jnp.broadcast_to(column, (cells, 128))

    pl.semaphore_wait(barrier, planes - 1 + jnp.where(place > 0, 1, 0) + jnp.where(place < last, 1, 0))

    def spread(r, s, source, target, send, recv):
        return pltpu.make_async_remote_copy(
            src_ref=source.at[peers[s], r], dst_ref=target.at[mine, r],
            send_sem=send.at[r, s], recv_sem=recv.at[r, s],
            device_id=(place, peers[s]), device_id_type=MESH)

    def sweep(b, n, source, target, send, recv, step):
        return pltpu.make_async_remote_copy(
            src_ref=source.at[b, n], dst_ref=target.at[b, n],
            send_sem=send.at[b, n], recv_sem=recv.at[b, n],
            device_id=(place + step, mine), device_id_type=MESH)

    def up(b, n):
        return sweep(b, n, ahead_out, ahead, ahead_send, ahead_recv, 1)

    def down(b, n):
        return sweep(b, n, behind_out, behind, behind_send, behind_recv, -1)

    for r in range(loads):
        for s in range(planes - 1):
            spread(r, s, stage, lines, in_send, in_recv).start()
        lines[mine, r] = stage[mine, r]

    chunk = width // CHUNKS

    def combine(left, right):
        real = left[:cells] - right[cells:]
        imag = right[:cells] + left[cells:]
        return real, imag

    def pack(real, imag):
        return jnp.concatenate([real, imag], axis=0)

    def dot(operand, k, start, size):
        return jnp.dot(operand, inverse[k * chunk:(k + 1) * chunk, start:start + size],
                       preferred_element_type=jnp.float32)

    def twist(b, real, imag):
        a = jnp.tile(factors[0, b], (1, chunk // 128))
        c = jnp.tile(factors[1, b], (1, chunk // 128))
        return a * real - c * imag, a * imag + c * real

    def product(source, b, copy, use):
        total = None
        for k in range(CHUNKS - 1):
            copy(b, k).wait_recv()
            term = dot(source[b, k], k, 0, 2 * width)
            total = term if total is None else total + term
        k = CHUNKS - 1
        copy(b, k).wait_recv()
        operand = source[b, k]
        for n in range(CHUNKS):
            left = dot(operand, k, n * chunk, chunk)
            right = dot(operand, k, width + n * chunk, chunk)
            if total is not None:
                left = total[:, n * chunk:(n + 1) * chunk] + left
                right = total[:, width + n * chunk:width + (n + 1) * chunk] + right
            use(n, *combine(left, right))

    def send_up(b, n, field):
        ahead_out[b, n] = field.astype(jnp.bfloat16)
        up(b, n).start()

    def send_down(b, n, real, imag):
        behind_out[b, n] = pack(*twist(b, real, imag)).astype(jnp.bfloat16)
        down(b, n).start()

    def keep(b, n, field):
        for p in range(n * chunk // part, (n + 1) * chunk // part):
            at = p * part - n * chunk
            out_stage[p, b] = field[:, at:at + part].astype(jnp.bfloat16)

    def finish(b):
        for s in range(planes - 1):
            spread(b, s, out_stage, out_in, out_send, out_recv).start()

    for b in range(loads):
        for s in range(planes - 1):
            spread(b, s, stage, lines, in_send, in_recv).wait_recv()
        if b == 0:
            load_inverse.wait()
        source = jnp.concatenate([lines[p, b] for p in range(planes)], axis=1)
        for n in range(CHUNKS):
            left = jnp.dot(source, inverse[:, n * chunk:(n + 1) * chunk], preferred_element_type=jnp.float32)
            right = jnp.dot(source, inverse[:, width + n * chunk:width + (n + 1) * chunk],
                            preferred_element_type=jnp.float32)
            field = pack(*combine(left, right))
            forward[b, n] = field

            @pl.when(place == 0)
            def _():
                send_up(b, n, field)

    @pl.when(place > 0)
    def _():
        for b in range(loads):
            def use(n, real, imag):
                real, imag = twist(b, real, imag)
                field = forward[b, n] + pack(real, imag)

                @pl.when(place < last)
                def _():
                    send_up(b, n, field)

                @pl.when(place == last)
                def _():
                    send_down(b, n, field[:cells], field[cells:])
                    keep(b, n, field)

                forward[b, n] = field

            product(ahead, b, up, use)

            @pl.when(place == last)
            def _():
                finish(b)

    @pl.when(place < last)
    def _():
        for b in range(loads):
            def use(n, real, imag):
                field = forward[b, n] + pack(real, imag)

                @pl.when(place > 0)
                def _():
                    send_down(b, n, field[:cells], field[cells:])

                keep(b, n, field)

            product(behind, b, down, use)
            finish(b)

    out_in[mine] = out_stage[mine]
    for r in range(loads):
        for s in range(planes - 1):
            spread(r, s, out_stage, out_in, out_send, out_recv).wait_recv()
        for p in range(planes):
            out[0, :, r, p * cells:(p + 1) * cells, :] = out_in[p, r].astype(jnp.float32).reshape(2, cells, part)

    for r in range(loads):
        for s in range(planes - 1):
            spread(r, s, stage, lines, in_send, in_recv).wait_send()
            spread(r, s, out_stage, out_in, out_send, out_recv).wait_send()

    @pl.when(place < last)
    def _():
        for b in range(loads):
            for n in range(CHUNKS):
                up(b, n).wait_send()

    @pl.when(place > 0)
    def _():
        for b in range(loads):
            for n in range(CHUNKS):
                down(b, n).wait_send()


def body(rhs_field, panel_inverse, coupling):
    layers, planes = lax.axis_size("layer"), lax.axis_size("plane")
    loads, part = rhs_field.shape[2], rhs_field.shape[4]
    width = panel_inverse.shape[1]
    cells = coupling.shape[3]
    rows = 2 * cells
    exchange = pltpu.VMEM((planes, loads, rows, part), jnp.bfloat16)
    hop = pltpu.VMEM((loads, CHUNKS, rows, width // CHUNKS), jnp.bfloat16)
    per_peer = pltpu.SemaphoreType.DMA((loads, planes - 1))
    per_block = pltpu.SemaphoreType.DMA((loads, CHUNKS))
    vmem = pl.BlockSpec(memory_space=pltpu.VMEM)
    return pl.pallas_call(
        functools.partial(kernel, layers, planes),
        out_shape=jax.ShapeDtypeStruct(rhs_field.shape, jnp.float32),
        in_specs=[vmem, pl.BlockSpec(memory_space=pl.ANY), vmem],
        out_specs=vmem,
        scratch_shapes=[
            pltpu.VMEM(panel_inverse.shape[1:], jnp.bfloat16),
            exchange,
            exchange,
            pltpu.VMEM((2, loads, cells, 128), jnp.float32),
            hop,
            hop,
            hop,
            hop,
            pltpu.VMEM((loads, CHUNKS, rows, width // CHUNKS), jnp.float32),
            exchange,
            exchange,
            pltpu.SemaphoreType.DMA,
            per_peer,
            per_peer,
            per_block,
            per_block,
            per_block,
            per_block,
            per_peer,
            per_peer,
        ],
        compiler_params=pltpu.CompilerParams(
            collective_id=0, has_side_effects=True, vmem_limit_bytes=60 * 1024 * 1024),
    )(rhs_field, panel_inverse, coupling)


def solution(mesh):
    in_specs = (
        P("layer", None, None, None, "plane"),
        P("layer", None, None),
        P("layer", None, None, "plane"),
    )
    out_specs = P("layer", None, None, None, "plane")
    return jax.shard_map(body, mesh=mesh, in_specs=in_specs, out_specs=out_specs, check_vma=False)
```

```python
import functools

import jax
import jax.numpy as jnp
from jax import lax
from jax.experimental import pallas as pl
from jax.experimental.pallas import tpu as pltpu
from jax.sharding import PartitionSpec as P

MESH = pl.DeviceIdType.MESH
CHUNKS = 2


def kernel(layers, planes, rhs_hbm, inverse_hbm, coupling_hbm, out, rhs, coupling, inverse, stage, lines, factors, ahead, ahead_out,
           behind, behind_out, forward, out_stage, out_in, load_sem, in_send, in_recv, ahead_send, ahead_recv,
           behind_send, behind_recv, out_send, out_recv):
    place = lax.axis_index("layer")
    mine = lax.axis_index("plane")
    last = layers - 1
    loads = rhs.shape[2]
    cells = coupling.shape[3]
    width = inverse.shape[0]
    part = rhs.shape[4]
    rows = 2 * cells

    load_rhs = pltpu.make_async_copy(rhs_hbm, rhs, load_sem.at[0])
    load_coupling = pltpu.make_async_copy(coupling_hbm, coupling, load_sem.at[1])
    load_inverse = pltpu.make_async_copy(inverse_hbm.at[0], inverse, load_sem.at[2])
    load_rhs.start()
    load_coupling.start()
    load_inverse.start()

    barrier = pltpu.get_barrier_semaphore()
    peers = [lax.rem(mine + s, planes) for s in range(1, planes)]
    for peer in peers:
        pl.semaphore_signal(barrier, inc=1, device_id=(place, peer), device_id_type=MESH)

    @pl.when(place > 0)
    def _():
        pl.semaphore_signal(barrier, inc=1, device_id=(place - 1, mine), device_id_type=MESH)

    @pl.when(place < last)
    def _():
        pl.semaphore_signal(barrier, inc=1, device_id=(place + 1, mine), device_id_type=MESH)

    load_rhs.wait()
    for p in range(planes):
        for r in range(loads):
            piece = rhs[0, :, r, p * cells:(p + 1) * cells, :].reshape(rows, part)
            stage[p, r] = piece.astype(jnp.bfloat16)

    pl.semaphore_wait(barrier, planes - 1 + jnp.where(place > 0, 1, 0) + jnp.where(place < last, 1, 0))

    def spread(r, s, source, target, send, recv):
        return pltpu.make_async_remote_copy(
            src_ref=source.at[peers[s], r], dst_ref=target.at[mine, r],
            send_sem=send.at[r, s], recv_sem=recv.at[r, s],
            device_id=(place, peers[s]), device_id_type=MESH)

    def sweep(b, n, source, target, send, recv, step):
        return pltpu.make_async_remote_copy(
            src_ref=source.at[b, n], dst_ref=target.at[b, n],
            send_sem=send.at[b, n], recv_sem=recv.at[b, n],
            device_id=(place + step, mine), device_id_type=MESH)

    def up(b, n):
        return sweep(b, n, ahead_out, ahead, ahead_send, ahead_recv, 1)

    def down(b, n):
        return sweep(b, n, behind_out, behind, behind_send, behind_recv, -1)

    for r in range(loads):
        for s in range(planes - 1):
            spread(r, s, stage, lines, in_send, in_recv).start()
        lines[mine, r] = stage[mine, r]

    chunk = width // CHUNKS

    def combine(left, right):
        real = left[:cells] - right[cells:]
        imag = right[:cells] + left[cells:]
        return real, imag

    def pack(real, imag):
        return jnp.concatenate([real, imag], axis=0)

    def dot(operand, k, start, size):
        return jnp.dot(operand, inverse[k * chunk:(k + 1) * chunk, start:start + size],
                       preferred_element_type=jnp.float32)

    def twist(b, real, imag):
        a = jnp.tile(factors[0, b], (1, chunk // 128))
        c = jnp.tile(factors[1, b], (1, chunk // 128))
        return a * real - c * imag, a * imag + c * real

    def product(source, b, copy, use):
        total = None
        for k in range(CHUNKS - 1):
            copy(b, k).wait_recv()
            term = dot(source[b, k], k, 0, 2 * width)
            total = term if total is None else total + term
        k = CHUNKS - 1
        copy(b, k).wait_recv()
        operand = source[b, k]
        for n in range(CHUNKS):
            left = dot(operand, k, n * chunk, chunk)
            right = dot(operand, k, width + n * chunk, chunk)
            if total is not None:
                left = total[:, n * chunk:(n + 1) * chunk] + left
                right = total[:, width + n * chunk:width + (n + 1) * chunk] + right
            use(n, *combine(left, right))

    def send_up(b, n, field):
        ahead_out[b, n] = field.astype(jnp.bfloat16)
        up(b, n).start()

    def send_down(b, n, real, imag):
        behind_out[b, n] = pack(*twist(b, real, imag)).astype(jnp.bfloat16)
        down(b, n).start()

    def keep(b, n, field):
        for p in range(n * chunk // part, (n + 1) * chunk // part):
            at = p * part - n * chunk
            out_stage[p, b] = field[:, at:at + part].astype(jnp.bfloat16)

    def finish(b):
        for s in range(planes - 1):
            spread(b, s, out_stage, out_in, out_send, out_recv).start()

    load_coupling.wait()
    eye = lax.broadcasted_iota(jnp.int32, (cells, cells), 0) == lax.broadcasted_iota(jnp.int32, (cells, cells), 1)
    for c in range(2):
        for r in range(loads):
            row = jnp.broadcast_to(coupling[0, c, r:r + 1, :], (cells, cells))
            column = jnp.sum(jnp.where(eye, row, 0.0), axis=1, keepdims=True)
            factors[c, r] = jnp.broadcast_to(column, (cells, 128))

    for b in range(loads):
        for s in range(planes - 1):
            spread(b, s, stage, lines, in_send, in_recv).wait_recv()
        if b == 0:
            load_inverse.wait()
        source = jnp.concatenate([lines[p, b] for p in range(planes)], axis=1)
        for n in range(CHUNKS):
            left = jnp.dot(source, inverse[:, n * chunk:(n + 1) * chunk], preferred_element_type=jnp.float32)
            right = jnp.dot(source, inverse[:, width + n * chunk:width + (n + 1) * chunk],
                            preferred_element_type=jnp.float32)
            field = pack(*combine(left, right))
            forward[b, n] = field

            @pl.when(place == 0)
            def _():
                send_up(b, n, field)

    @pl.when((place > 0) & (place < last))
    def _():
        for b in range(loads):
            def use(n, real, imag):
                field = forward[b, n] + pack(*twist(b, real, imag))
                send_up(b, n, field)
                forward[b, n] = field

            product(ahead, b, up, use)

    @pl.when(place == last)
    def _():
        for b in range(loads):
            def use(n, real, imag):
                field = forward[b, n] + pack(*twist(b, real, imag))
                send_down(b, n, field[:cells], field[cells:])
                keep(b, n, field)

            product(ahead, b, up, use)
            finish(b)

    @pl.when((place > 0) & (place < last))
    def _():
        for b in range(loads):
            def use(n, real, imag):
                field = forward[b, n] + pack(real, imag)
                send_down(b, n, field[:cells], field[cells:])
                keep(b, n, field)

            product(behind, b, down, use)
            finish(b)

    @pl.when(place == 0)
    def _():
        for b in range(loads):
            def use(n, real, imag):
                keep(b, n, forward[b, n] + pack(real, imag))

            product(behind, b, down, use)
            finish(b)

    out_in[mine] = out_stage[mine]
    for r in range(loads):
        for s in range(planes - 1):
            spread(r, s, out_stage, out_in, out_send, out_recv).wait_recv()
        for p in range(planes):
            out[0, :, r, p * cells:(p + 1) * cells, :] = out_in[p, r].astype(jnp.float32).reshape(2, cells, part)

    for r in range(loads):
        for s in range(planes - 1):
            spread(r, s, stage, lines, in_send, in_recv).wait_send()
            spread(r, s, out_stage, out_in, out_send, out_recv).wait_send()

    @pl.when(place < last)
    def _():
        for b in range(loads):
            for n in range(CHUNKS):
                up(b, n).wait_send()

    @pl.when(place > 0)
    def _():
        for b in range(loads):
            for n in range(CHUNKS):
                down(b, n).wait_send()


def body(rhs_field, panel_inverse, coupling):
    layers, planes = lax.axis_size("layer"), lax.axis_size("plane")
    loads, part = rhs_field.shape[2], rhs_field.shape[4]
    width = panel_inverse.shape[1]
    cells = coupling.shape[3]
    rows = 2 * cells
    exchange = pltpu.VMEM((planes, loads, rows, part), jnp.bfloat16)
    hop = pltpu.VMEM((loads, CHUNKS, rows, width // CHUNKS), jnp.bfloat16)
    per_peer = pltpu.SemaphoreType.DMA((loads, planes - 1))
    per_block = pltpu.SemaphoreType.DMA((loads, CHUNKS))
    vmem = pl.BlockSpec(memory_space=pltpu.VMEM)
    return pl.pallas_call(
        functools.partial(kernel, layers, planes),
        out_shape=jax.ShapeDtypeStruct(rhs_field.shape, jnp.float32),
        in_specs=[pl.BlockSpec(memory_space=pl.ANY)] * 3,
        out_specs=vmem,
        scratch_shapes=[
            pltpu.VMEM(rhs_field.shape, jnp.float32),
            pltpu.VMEM(coupling.shape, jnp.float32),
            pltpu.VMEM(panel_inverse.shape[1:], jnp.bfloat16),
            exchange,
            exchange,
            pltpu.VMEM((2, loads, cells, 128), jnp.float32),
            hop,
            hop,
            hop,
            hop,
            pltpu.VMEM((loads, CHUNKS, rows, width // CHUNKS), jnp.float32),
            exchange,
            exchange,
            pltpu.SemaphoreType.DMA((3,)),
            per_peer,
            per_peer,
            per_block,
            per_block,
            per_block,
            per_block,
            per_peer,
            per_peer,
        ],
        compiler_params=pltpu.CompilerParams(
            collective_id=0, has_side_effects=True, vmem_limit_bytes=60 * 1024 * 1024),
    )(rhs_field, panel_inverse, coupling)


def solution(mesh):
    in_specs = (
        P("layer", None, None, None, "plane"),
        P("layer", None, None),
        P("layer", None, None, "plane"),
    )
    out_specs = P("layer", None, None, None, "plane")
    return jax.shard_map(body, mesh=mesh, in_specs=in_specs, out_specs=out_specs, check_vma=False)
```
